128 devices in a mesh: gx: 8 (over x, z_hi), gy: 16 (over z_lo, y, core).
Axes of the slice: x: 4, y: 4, z: 4 (z_hi: 2, z_lo: 2; z = z_hi * 2 + z_lo), core: 2. Of those that a mesh axis runs over, the one named last changes fastest.
Arguments:
- density: bfloat16 [4, 64, 16384], P(None, 'gx', 'gy'), may hold values from -6 to 6
- weight_one: bfloat16 [64, 108], replicated, may hold values from -0.625 to 0.625
- weight_two: bfloat16 [256, 1728], P('gx'), may hold values from -0.15625 to 0.15625
- feature_cot: bfloat16 [256, 32, 4096], P('gx', 'gy'), may hold values from -0.0390625 to 0.0390625
Outputs:
- features: bfloat16 [256, 32, 4096], P('gx', 'gy')
- grad_one: float32 [64, 108], replicated
- grad_two: float32 [256, 1728], P('gx')
The draws below stay inside these ranges and needn't reach their ends.
All inputs are finite; a program needn't handle non-finite values.
Results may differ from the reference program's by a relative error of at most 0.025.
Values may be sent and summed in bfloat16 or wider, within the bound.
No kernel may reach another device: no remote copies, remote signals or barrier semaphores. Data moves between devices by JAX's collectives and lax.ppermute only.
A program may use at most 128 MiB of HBM per device.

```python
import jax
import jax.numpy as jnp
from jax import lax

C0 = 4
C1 = 64
C2 = 256
Z = 64
NX = 64
NY = 256


def shard_levels(own_key, shape, shards, low, largest):
    def one(axis_at, parts):
        steps = jax.random.uniform(jax.random.fold_in(jax.random.fold_in(own_key, 6), axis_at), (parts,), jnp.float32, low / len(shards), largest / len(shards))
        return jnp.repeat(jnp.exp(steps), shape[axis_at] // parts).reshape((-1,) + (1,) * (len(shape) - axis_at - 1))

    gain = one(*shards[0])
    for cut in shards[1:]:
        gain = gain * one(*cut)
    return gain


def centred(key, shape, deviation, limit, shards=(), held_as=jnp.bfloat16):
    gain = shard_levels(key, shape, shards, -0.22, 0.18) if shards else 1.0
    entries = jax.random.normal(key, shape, jnp.float32) * deviation * gain
    return jnp.minimum(jnp.maximum(entries, -limit), limit).astype(held_as)


def setup_inputs(seed: int = 0) -> dict:
    seeds = jax.random.split(jax.random.key(seed), 5)
    return {
        "density": centred(seeds[0], (C0, NX, NY * Z), 1.0, 6.0, ((1, 8), (2, 16))),
        "weight_one": centred(seeds[1], (C1, 27 * C0), (27 * C0) ** -0.5, 0.625),
        "weight_two": centred(seeds[2], (C2, 27 * C1), (27 * C1) ** -0.5, 0.15625, ((0, 8),)),
        "feature_cot": centred(seeds[3], (C2, NX // 2, (NY // 2) * (Z // 2)), ((NX * NY * Z // 8) ** -0.5), 0.0390625, ((0, 8), (1, 16))),
    }


def leaky_relu(values):
    return values * (0.65 + 0.35 * jnp.tanh(values))


def relu_slope(values):
    bent = jnp.tanh(values)
    return 0.65 + 0.35 * bent + 0.35 * values * (1.0 - bent * bent)


def kernel_of(weight, inputs):
    outputs = weight.shape[0]
    return weight.reshape(outputs, 3, 3, 3, inputs).transpose(0, 4, 1, 2, 3)


def flipped(kernel):
    return jnp.flip(kernel, (2, 3, 4)).transpose(1, 0, 2, 3, 4)


def periodic_pad(values):
    wrapped = jnp.pad(values, ((0, 0), (1, 1), (1, 1), (0, 0)), mode="wrap")
    return jnp.pad(wrapped, ((0, 0), (0, 0), (0, 0), (1, 1)))


def conv_valid(padded, kernel):
    result = lax.conv_general_dilated(padded[None], kernel, (1, 1, 1), "VALID",
                                      dimension_numbers=("NCDHW", "OIDHW", "NCDHW"),
                                      preferred_element_type=jnp.float32)
    return result[0]


def tap_grads(padded, grad_cells):
    outputs, size_x, size_y, size_z = grad_cells.shape
    pieces = []
    for step_x in range(3):
        for step_y in range(3):
            for step_z in range(3):
                window = padded[:, step_x:step_x + size_x, step_y:step_y + size_y, step_z:step_z + size_z]
                pieces.append(jnp.einsum("oxyz,ixyz->oi", grad_cells, window))
    stacked = jnp.stack(pieces, axis=1)
    return stacked.reshape(outputs, -1)


def reference(density, weight_one, weight_two, feature_cot):
    volume = density.reshape(C0, NX, NY, Z).astype(jnp.float32)
    padded_one = periodic_pad(volume)
    pre_one = conv_valid(padded_one, kernel_of(weight_one.astype(jnp.float32), C0))
    act_one = leaky_relu(pre_one)
    pooled = act_one.reshape(C1, NX // 2, 2, NY // 2, 2, Z // 2, 2).mean(axis=(2, 4, 6)).astype(jnp.bfloat16)
    pooled_wide = pooled.astype(jnp.float32)
    padded_two = periodic_pad(pooled_wide)
    kernel_two = kernel_of(weight_two.astype(jnp.float32), C1)
    pre_two = conv_valid(padded_two, kernel_two)
    features = leaky_relu(pre_two).astype(jnp.bfloat16).reshape(C2, NX // 2, (NY // 2) * (Z // 2))
    cotangent = feature_cot.reshape(C2, NX // 2, NY // 2, Z // 2).astype(jnp.float32)
    grads_two = (cotangent * relu_slope(pre_two)).astype(jnp.bfloat16)
    grads_two = lax.optimization_barrier(grads_two).astype(jnp.float32)
    grad_two = tap_grads(padded_two, grads_two)
    pooled_grad = conv_valid(periodic_pad(grads_two), flipped(kernel_two)).astype(jnp.bfloat16)
    grown = jnp.repeat(jnp.repeat(jnp.repeat(pooled_grad, 2, 1), 2, 2), 2, 3).astype(jnp.float32)
    grads_one = (grown * (0.125 * relu_slope(pre_one))).astype(jnp.bfloat16)
    grads_one = lax.optimization_barrier(grads_one).astype(jnp.float32)
    grad_one = tap_grads(padded_one, grads_one)
    return features, grad_one, grad_two
```

```python
import jax
import jax.numpy as jnp
import numpy as np
from jax import lax
from jax.experimental import pallas as pl
from jax.experimental.pallas import tpu as pltpu
from jax.sharding import PartitionSpec as P

C0 = 4
C1 = 64
Z = 64
HZ = 32
CELLS = 4096
ROWS = 4
TILE = 512
F32 = jnp.float32
BF16 = jnp.bfloat16


def split_depth():
    sort = np.zeros((1024, 1024), np.float32)
    for y in range(16):
        for z in range(Z):
            sort[y * Z + z, ((y % 2) * 2 + z % 2) * 256 + (y // 2) * HZ + z // 2] = 1
    return sort


def window_taps():
    place = {(1, 1): 0, (0, 0): 1, (0, 1): 2, (1, 0): 3}
    taps = np.zeros((8, 256, 128), np.float32)
    for cell in range(8):
        a, b, c = cell // 4, cell // 2 % 2, cell % 2
        for x in range(4):
            for y_key, y in place.items():
                for z_key, z in place.items():
                    dx, dy, dz = x - a, y - b, z - c
                    if min(dx, dy, dz) < 0 or max(dx, dy, dz) > 2:
                        continue
                    row = x * 64 + y_key[0] * 32 + z_key[0] * 16 + y_key[1] * 8 + z_key[1] * 4
                    for i in range(C0):
                        taps[cell, row + i, (9 * dx + 3 * dy + dz) * C0 + i] = 1
    return taps


def depth_of(shape):
    return lax.broadcasted_iota(jnp.int32, shape, 1) % HZ


def move(values, step):
    return pltpu.roll(values, step % values.shape[1], 1)


def from_below(values, depth):
    return jnp.where(depth != 0, move(values, 1), 0.0)


def from_above(values, depth):
    return jnp.where(depth != HZ - 1, move(values, -1), 0.0)


def fine_kernel(parts_ref, weight_ref, windows_ref, pooled_ref, slope_ref):
    row, tile = pl.program_id(0), pl.program_id(1)

    @pl.when((row == 0) & (tile == 0))
    def _():
        depth = depth_of((8, CELLS))
        low = lax.broadcasted_iota(jnp.int32, (8, CELLS), 0) < 4
        for x in range(10):
            cells = jnp.concatenate(
                [parts_ref[c, 16 * x : 16 * x + 16, :] for c in range(8)], axis=1
            ).astype(F32)
            even, odd = cells[:8], cells[8:]
            for shifted, (top, bottom) in enumerate(
                ((even, odd), (move(even, -HZ), move(odd, HZ)))
            ):
                at = 64 * x + 32 * shifted
                windows_ref[at : at + 16, :] = jnp.concatenate([top, bottom], axis=0).astype(BF16)
                moved = [
                    jnp.where(low, from_above(half, depth), from_below(half, depth))
                    for half in (top, bottom)
                ]
                windows_ref[at + 16 : at + 32, :] = jnp.concatenate(moved, axis=0).astype(BF16)

    lanes = pl.ds(pl.multiple_of(tile * TILE, TILE), TILE)
    window = windows_ref[pl.ds(pl.multiple_of(row * 128, 128), 256), lanes]
    pre = jnp.dot(weight_ref[...], window, preferred_element_type=F32)
    total = None
    for cell in range(8):
        value = pre[C1 * cell : C1 * cell + C1].astype(BF16)
        bent = jnp.tanh(value)
        gate = bent * 0.35 + 0.65
        act = value * gate
        slope_ref[0, C1 * cell : C1 * cell + C1, :] = gate + (value * 0.35) * (1.0 - bent * bent)
        total = act.astype(F32) if total is None else total + act.astype(F32)
    pooled_ref[...] = (total * 0.125).astype(BF16)


def coarse_kernel(pooled_ref, forward_ref, backward_ref, cot_ref, feature_ref, back_ref, grad_ref, wide_ref, moved_ref):
    for tile in range(CELLS // TILE):
        lanes = slice(tile * TILE, tile * TILE + TILE)
        wide_ref[:, lanes] = jnp.dot(forward_ref[...], pooled_ref[:, lanes], preferred_element_type=F32)
    depth = depth_of((16, CELLS))
    for block in range(4):
        def term(dy, dz):
            at = 64 * (3 * dy + dz) + 16 * block
            return wide_ref[at : at + 16, :]

        def column(dz):
            return term(1, dz) + move(term(0, dz), HZ) + move(term(2, dz), -HZ)

        pre = column(1) + from_below(column(0), depth) + from_above(column(2), depth)
        rows = slice(16 * block, 16 * block + 16)
        bent = jnp.tanh(pre)
        gate = 0.65 + 0.35 * bent
        feature_ref[rows, :] = (pre * gate).astype(BF16)
        slope = gate + 0.35 * pre * (1.0 - bent * bent)
        grads = (cot_ref[rows, :].astype(F32) * slope).astype(BF16).astype(F32)
        for dy in range(3):
            here = grads if dy == 1 else move(grads, HZ * (dy - 1))
            for dz in range(3):
                there = here if dz == 1 else (from_above if dz == 0 else from_below)(here, depth)
                at = 64 * (3 * dy + dz) + 16 * block
                moved_ref[at : at + 16, :] = there.astype(BF16)
    for tile in range(CELLS // TILE):
        lanes = slice(tile * TILE, tile * TILE + TILE)
        back_ref[:, lanes] = jnp.dot(
            backward_ref[...], moved_ref[:, lanes], preferred_element_type=F32
        ).astype(BF16)
    grad = lax.dot_general(
        moved_ref[...], pooled_ref[...], (((1,), (1,)), ((), ())), preferred_element_type=F32
    )
    for tap in range(9):
        both = grad[64 * tap : 64 * tap + 32, :192] + grad[64 * tap + 32 : 64 * tap + 64, 64:]
        for dx in range(3):
            at = dx * 576 + tap * 64
            grad_ref[:, at : at + 64] = both[:, 64 * dx : 64 * dx + 64].astype(BF16)


def fine_back_kernel(windows_ref, slope_ref, back_ref, taps_ref, grad_ref, sum_ref):
    row, tile = pl.program_id(0), pl.program_id(1)
    lanes = pl.ds(pl.multiple_of(tile * TILE, TILE), TILE)
    window = windows_ref[pl.ds(pl.multiple_of(row * 128, 128), 256), lanes]
    back = back_ref[...]
    grads = jnp.concatenate(
        [slope_ref[0, C1 * cell : C1 * cell + C1, :] * back for cell in range(8)], axis=0
    )
    term = lax.dot_general(grads, window, (((1,), (1,)), ((), ())), preferred_element_type=F32)
    first = (row == 0) & (tile == 0)

    @pl.when(first)
    def _():
        sum_ref[...] = term

    @pl.when(jnp.logical_not(first))
    def _():
        sum_ref[...] += term

    @pl.when((row == ROWS - 1) & (tile == CELLS // TILE - 1))
    def _():
        total = jnp.zeros((C1, 128), F32)
        for cell in range(8):
            whole = sum_ref[C1 * cell : C1 * cell + C1, :]
            high = whole.astype(BF16)
            low = (whole - high.astype(F32)).astype(BF16)
            total += jnp.dot(high, taps_ref[cell], preferred_element_type=F32)
            total += jnp.dot(low, taps_ref[cell], preferred_element_type=F32)
        grad_ref[...] = total * 0.125


def fine_forward(parts, weight):
    return pl.pallas_call(
        fine_kernel,
        grid=(ROWS, CELLS // TILE),
        in_specs=[
            pl.BlockSpec((8, 160, 512), lambda r, t: (0, 0, 0)),
            pl.BlockSpec((512, 256), lambda r, t: (0, 0)),
        ],
        out_specs=[
            pl.BlockSpec((640, CELLS), lambda r, t: (0, 0)),
            pl.BlockSpec((C1, TILE), lambda r, t: (r, t)),
            pl.BlockSpec((1, 512, TILE), lambda r, t: (r, 0, t)),
        ],
        out_shape=[
            jax.ShapeDtypeStruct((640, CELLS), BF16),
            jax.ShapeDtypeStruct((ROWS * C1, CELLS), BF16),
            jax.ShapeDtypeStruct((ROWS, 512, CELLS), BF16),
        ],
        compiler_params=pltpu.CompilerParams(vmem_limit_bytes=40 << 20),
        name="fine_forward",
    )(parts, weight)


def coarse(pooled, forward, backward, cot):
    whole = pl.BlockSpec(memory_space=pltpu.VMEM)
    return pl.pallas_call(
        coarse_kernel,
        in_specs=[whole] * 4,
        out_specs=[whole] * 3,
        out_shape=[
            jax.ShapeDtypeStruct((64, CELLS), BF16),
            jax.ShapeDtypeStruct((256, CELLS), BF16),
            jax.ShapeDtypeStruct((32, 1728), BF16),
        ],
        scratch_shapes=[pltpu.VMEM((576, CELLS), F32), pltpu.VMEM((576, CELLS), BF16)],
        compiler_params=pltpu.CompilerParams(vmem_limit_bytes=48 << 20),
        name="coarse",
    )(pooled, forward, backward, cot)


def fine_backward(windows, slope, back, taps):
    return pl.pallas_call(
        fine_back_kernel,
        grid=(ROWS, CELLS // TILE),
        in_specs=[
            pl.BlockSpec((640, CELLS), lambda r, t: (0, 0)),
            pl.BlockSpec((1, 512, TILE), lambda r, t: (r, 0, t)),
            pl.BlockSpec((C1, TILE), lambda r, t: (r, t)),
            pl.BlockSpec((8, 256, 128), lambda r, t: (0, 0, 0)),
        ],
        out_specs=pl.BlockSpec((C1, 128), lambda r, t: (0, 0)),
        out_shape=jax.ShapeDtypeStruct((C1, 128), F32),
        scratch_shapes=[pltpu.VMEM((512, 256), F32)],
        compiler_params=pltpu.CompilerParams(vmem_limit_bytes=40 << 20),
        name="fine_backward",
    )(windows, slope, back, taps)


def strip_part(density):
    sort = jnp.asarray(split_depth(), BF16)
    sorted_cells = jnp.dot(density.reshape(32, 1024), sort, preferred_element_type=F32).astype(BF16)
    block = sorted_cells.reshape(C0, 8, 4, 256).transpose(1, 2, 0, 3).reshape(8, 16, 256)
    side = lax.axis_index("gy") % 2
    both = [(gx, gy) for gx in range(8) for gy in range(16)]

    def send(values, target):
        pairs = []
        for gx, gy in both:
            to_x, to_y = target(gx, gy)
            pairs.append((gx * 16 + gy, to_x * 16 + to_y % 16))
        return lax.ppermute(values, ("gx", "gy"), pairs)

    main = [block[0:7], block[1:8]]
    rim = [block[5:8], block[0:3]]
    even = side == 0
    same = send(jnp.where(even, main[0], main[1]), lambda gx, gy: (gy // 2, 2 * gx + gy % 2))
    other = send(jnp.where(even, main[1], main[0]), lambda gx, gy: (gy // 2, 2 * gx + 1 - gy % 2))
    rim_same = send(
        jnp.where(even, rim[0], rim[1]),
        lambda gx, gy: (gy // 2, 2 * gx + 2 if gy % 2 == 0 else 2 * gx - 1),
    )
    rim_other = send(
        jnp.where(even, rim[1], rim[0]),
        lambda gx, gy: (gy // 2, 2 * gx - 1 if gy % 2 == 0 else 2 * gx + 2),
    )
    lower = jnp.concatenate(
        [jnp.concatenate([rim_same, same], 0), jnp.concatenate([rim_other, other], 0)], 2
    )
    upper = jnp.concatenate(
        [jnp.concatenate([other, rim_other], 0), jnp.concatenate([same, rim_same], 0)], 2
    )
    return jnp.where(even, lower, upper).reshape(160, 512)


def coarse_weights(weight_two):
    taps = weight_two.reshape(32, 3, 9, C1)
    both = jnp.stack([jnp.pad(taps, ((0, 0), (r, 1 - r), (0, 0), (0, 0))) for r in range(2)])
    forward = both.transpose(3, 0, 1, 2, 4).reshape(576, 256)
    return forward, forward.T


def body(density, weight_one, weight_two, feature_cot):
    taps = jnp.asarray(window_taps(), BF16)
    with jax.named_scope("strip"):
        part = strip_part(density)
        parts = lax.all_to_all(jnp.broadcast_to(part[None], (8, 160, 512)), "gx", 0, 0)
    with jax.named_scope("weights"):
        fine_weight = jnp.einsum(
            "ok,srk->sor", jnp.pad(weight_one, ((0, 0), (0, 20))), taps, preferred_element_type=F32
        ).astype(BF16).reshape(512, 256)
        forward, backward = coarse_weights(weight_two)
        cot = feature_cot.transpose(1, 0, 2).reshape(64, CELLS)
    windows, pooled, slope = fine_forward(parts, fine_weight)
    features, back, grad_two = coarse(pooled, forward, backward, cot)
    features = features.reshape(2, 32, CELLS).transpose(1, 0, 2)
    with jax.named_scope("sum_two"):
        terms = lax.all_to_all(grad_two.reshape(16, 2, 1728), "gy", 0, 0)
        mine = terms.astype(F32).sum(0).astype(BF16)
        grad_two = lax.all_to_all(jnp.broadcast_to(mine[None], (16, 2, 1728)), "gy", 0, 0)
        grad_two = grad_two.reshape(32, 1728).astype(F32)
    grad_one = fine_backward(windows, slope, back, taps)
    with jax.named_scope("sum_one"):
        terms = lax.all_to_all(grad_one.reshape(16, 4, 128), "gy", 0, 0)
        mine = terms.sum(0)
        whole = lax.all_to_all(jnp.broadcast_to(mine[None], (128, 4, 128)), ("gx", "gy"), 0, 0)
        grad_one = whole.reshape(8, 64, 128).sum(0)[:, :108]
    return features, grad_one, grad_two


def solution(mesh):
    return jax.shard_map(
        body,
        mesh=mesh,
        in_specs=(P(None, "gx", "gy"), P(), P("gx", None), P("gx", "gy", None)),
        out_specs=(P("gx", "gy", None), P(), P("gx", None)),
        check_vma=False,
    )
```

```python
import jax
import jax.numpy as jnp
import numpy as np
from jax import lax
from jax.experimental import pallas as pl
from jax.experimental.pallas import tpu as pltpu
from jax.sharding import Mesh, PartitionSpec as P

C0 = 4
C1 = 64
Z = 64
HZ = 32
CELLS = 4096
ROWS = 4
TILE = 512
WIDE = 2048
CHIP = ("x", "zh", "zl", "y", "core")
F32 = jnp.float32
BF16 = jnp.bfloat16


def split_depth():
    sort = np.zeros((1024, 1024), np.float32)
    for y in range(16):
        for z in range(Z):
            sort[y * Z + z, ((y % 2) * 2 + z % 2) * 256 + (y // 2) * HZ + z // 2] = 1
    return sort


def window_taps():
    place = {(1, 1): 0, (0, 0): 1, (0, 1): 2, (1, 0): 3}
    taps = np.zeros((8, 256, 128), np.float32)
    for cell in range(8):
        a, b, c = cell // 4, cell // 2 % 2, cell % 2
        for x in range(4):
            for y_key, y in place.items():
                for z_key, z in place.items():
                    dx, dy, dz = x - a, y - b, z - c
                    if min(dx, dy, dz) < 0 or max(dx, dy, dz) > 2:
                        continue
                    row = x * 64 + y_key[0] * 32 + z_key[0] * 16 + y_key[1] * 8 + z_key[1] * 4
                    for i in range(C0):
                        taps[cell, row + i, (9 * dx + 3 * dy + dz) * C0 + i] = 1
    return taps


def depth_of(shape):
    return lax.broadcasted_iota(jnp.int32, shape, 1) % HZ


def move(values, step):
    return pltpu.roll(values, step % values.shape[1], 1)


def from_below(values, depth):
    return jnp.where(depth != 0, move(values, 1), 0.0)


def from_above(values, depth):
    return jnp.where(depth != HZ - 1, move(values, -1), 0.0)


def place_windows(cells, windows_ref, at):
    depth = depth_of((8, CELLS))
    low = lax.broadcasted_iota(jnp.int32, (8, CELLS), 0) < 4
    cells = cells.astype(F32)
    even, odd = cells[:8], cells[8:]
    for shifted, (top, bottom) in enumerate(((even, odd), (move(even, -HZ), move(odd, HZ)))):
        here = pl.multiple_of(at + 32 * shifted, 32)
        windows_ref[pl.ds(here, 16), :] = jnp.concatenate([top, bottom], axis=0).astype(BF16)
        moved = [
            jnp.where(low, from_above(half, depth), from_below(half, depth))
            for half in (top, bottom)
        ]
        windows_ref[pl.ds(here + 16, 16), :] = jnp.concatenate(moved, axis=0).astype(BF16)


def levels_kernel(
    side_ref, own_ref, other_ref, fine_ref, forward_ref, backward_ref, cot_ref, taps_ref,
    feature_ref, grad_ref,
    windows_ref, slope_ref, pooled_ref, wide_ref, moved_ref, back_ref, sum_ref,
):
    side = side_ref[0]

    def row_of(ref, j):
        return jnp.concatenate([ref[c, 16 * j : 16 * j + 16, :] for c in range(8)], axis=1)

    for j in range(4):
        place_windows(row_of(own_ref, j), windows_ref, 64 * (3 + j))
    for j in range(3):
        place_windows(row_of(own_ref, 4 + j), windows_ref, 64 * (j + 7 * side))
        place_windows(row_of(other_ref, j), windows_ref, 64 * (j + 7 * (1 - side)))

    def fine_step(step, _):
        row, tile = step // (CELLS // WIDE), step % (CELLS // WIDE)
        lanes = pl.ds(pl.multiple_of(tile * WIDE, WIDE), WIDE)
        window = windows_ref[pl.ds(pl.multiple_of(row * 128, 128), 256), lanes]
        pre = jnp.dot(fine_ref[...], window, preferred_element_type=F32)
        total = None
        for cell in range(8):
            value = pre[C1 * cell : C1 * cell + C1].astype(BF16)
            bent = jnp.tanh(value)
            gate = bent + 0.65 / 0.35
            act = value * gate
            slope_ref[row * 8 + cell, :, lanes] = gate + value * (1.0 - bent * bent)
            total = act if total is None else total + act
        pooled_ref[pl.ds(pl.multiple_of(row * C1, C1), C1), lanes] = (
            total.astype(F32) * (0.125 * 0.35)
        ).astype(BF16)
        return 0

    lax.fori_loop(0, ROWS * CELLS // WIDE, fine_step, 0)

    for tile in range(CELLS // TILE):
        lanes = slice(tile * TILE, tile * TILE + TILE)
        wide_ref[:, lanes] = jnp.dot(forward_ref[...], pooled_ref[:, lanes], preferred_element_type=F32)
    depth = depth_of((16, CELLS))
    for block in range(4):
        def term(dy, dz):
            at = 64 * (3 * dy + dz) + 16 * block
            return wide_ref[at : at + 16, :]

        def column(dz):
            return term(1, dz) + move(term(0, dz), HZ) + move(term(2, dz), -HZ)

        pre = column(1) + from_below(column(0), depth) + from_above(column(2), depth)
        rows = slice(16 * block, 16 * block + 16)
        bent = jnp.tanh(pre)
        gate = 0.65 + 0.35 * bent
        feature_ref[rows, :] = (pre * gate).astype(BF16)
        slope = gate + 0.35 * pre * (1.0 - bent * bent)
        grads = (cot_ref[rows, :].astype(F32) * slope).astype(BF16).astype(F32)
        for dy in range(3):
            here = grads if dy == 1 else move(grads, HZ * (dy - 1))
            for dz in range(3):
                there = here if dz == 1 else (from_above if dz == 0 else from_below)(here, depth)
                at = 64 * (3 * dy + dz) + 16 * block
                moved_ref[at : at + 16, :] = there.astype(BF16)
    for tile in range(CELLS // TILE):
        lanes = slice(tile * TILE, tile * TILE + TILE)
        back_ref[:, lanes] = jnp.dot(
            backward_ref[...], moved_ref[:, lanes], preferred_element_type=F32
        ).astype(BF16)
    grad = lax.dot_general(
        moved_ref[...], pooled_ref[...], (((1,), (1,)), ((), ())), preferred_element_type=F32
    )
    for tap in range(9):
        both = grad[64 * tap : 64 * tap + 32, :192] + grad[64 * tap + 32 : 64 * tap + 64, 64:]
        for dx in range(3):
            at = dx * 576 + tap * 64
            grad_ref[:, at : at + 64] = both[:, 64 * dx : 64 * dx + 64]
    grad_ref[:, 1728:1792] = jnp.zeros((32, 64), F32)

    sum_ref[...] = jnp.zeros_like(sum_ref)

    def back_step(row, _):
        window = windows_ref[pl.ds(pl.multiple_of(row * 128, 128), 256), :]
        back = back_ref[pl.ds(pl.multiple_of(row * C1, C1), C1), :]
        grads = jnp.concatenate([slope_ref[row * 8 + cell] * back for cell in range(8)], axis=0)
        sum_ref[...] += lax.dot_general(
            grads, window, (((1,), (1,)), ((), ())), preferred_element_type=F32
        )
        return 0

    lax.fori_loop(0, ROWS, back_step, 0)
    total = jnp.zeros((C1, 128), F32)
    for cell in range(8):
        whole = sum_ref[C1 * cell : C1 * cell + C1, :]
        high = whole.astype(BF16)
        low = (whole - high.astype(F32)).astype(BF16)
        total += jnp.dot(high, taps_ref[cell], preferred_element_type=F32)
        total += jnp.dot(low, taps_ref[cell], preferred_element_type=F32)
    total = total * (0.125 * 0.35)
    for half in range(2):
        for part in range(2):
            at = 32 * half + 16 * part
            grad_ref[16 * half : 16 * half + 16, 1792 + 128 * part : 1920 + 128 * part] = total[at : at + 16]


def levels(side, own, other, fine, forward, backward, cot, taps):
    whole = pl.BlockSpec(memory_space=pltpu.VMEM)
    return pl.pallas_call(
        levels_kernel,
        in_specs=[pl.BlockSpec(memory_space=pltpu.SMEM)] + [whole] * 7,
        out_specs=[whole] * 2,
        out_shape=[
            jax.ShapeDtypeStruct((64, CELLS), BF16),
            jax.ShapeDtypeStruct((32, 2048), F32),
        ],
        scratch_shapes=[
            pltpu.VMEM((640, CELLS), BF16),
            pltpu.VMEM((32, C1, CELLS), BF16),
            pltpu.VMEM((ROWS * C1, CELLS), BF16),
            pltpu.VMEM((576, CELLS), F32),
            pltpu.VMEM((576, CELLS), BF16),
            pltpu.VMEM((ROWS * C1, CELLS), BF16),
            pltpu.VMEM((512, 256), F32),
        ],
        compiler_params=pltpu.CompilerParams(vmem_limit_bytes=58 << 20),
        name="levels",
    )(side, own, other, fine, forward, backward, cot, taps)


def swap(values):
    return lax.ppermute(values, "core", [(0, 1), (1, 0)])


def by_core(side, mine, other, dim):
    return jnp.where(
        side == 0, jnp.concatenate([mine, other], dim), jnp.concatenate([other, mine], dim)
    )


def pair_list(target):
    pairs = []
    for gx in range(8):
        for chip in range(8):
            for core in range(2):
                to_x, to_chip, to_core = target(gx, chip, core)
                pairs.append(((gx * 8 + chip) * 2 + core, (to_x * 8 + to_chip % 8) * 2 + to_core))
    return pairs


def strip_parts(density, side):
    sort = jnp.asarray(split_depth(), BF16)
    sorted_cells = jnp.dot(density.reshape(32, 1024), sort, preferred_element_type=F32).astype(BF16)
    block = sorted_cells.reshape(C0, 8, 4, 256).transpose(1, 2, 0, 3).reshape(8, 16, 256)
    kept = jnp.where(side == 0, block[:4], block[4:])
    half = by_core(side, kept, swap(jnp.where(side == 0, block[4:], block[:4])), 2)
    main = lax.ppermute(half, CHIP, pair_list(lambda gx, chip, core: (chip, gx, core)))
    rim = lax.ppermute(
        jnp.where(side == 0, half[:3], half[1:]),
        CHIP,
        pair_list(lambda gx, chip, core: (chip, gx + 2 * core - 1, 1 - core)),
    )
    part = jnp.concatenate([main, rim], 0).reshape(112, 512)
    own = lax.all_to_all(jnp.broadcast_to(part[None], (8, 112, 512)), ("x", "zh"), 0, 0)
    other = swap(jnp.where(side == 0, own[:, 16:64], own[:, :48]))
    return own, other


def coarse_weights(weight_two):
    taps = weight_two.reshape(32, 3, 9, C1)
    both = jnp.stack([jnp.pad(taps, ((0, 0), (r, 1 - r), (0, 0), (0, 0))) for r in range(2)])
    forward = both.transpose(3, 0, 1, 2, 4).reshape(576, 256)
    return forward, forward.T


def sum_grads(terms, side):
    mine = jnp.where(side == 0, terms[:16], terms[16:])
    mine = mine + swap(jnp.where(side == 0, terms[16:], terms[:16]))
    copies = jnp.broadcast_to(mine.astype(BF16)[None], (8, 16, 2048))
    summed = lax.all_to_all(copies, ("zl", "y"), 0, 0).astype(F32).sum(0)
    copies = jnp.broadcast_to(summed[None, :, 1792:], (8, 16, 256))
    one = lax.all_to_all(copies, ("x", "zh"), 0, 0).sum(0)
    grad_two = by_core(side, summed[:, :1728], swap(summed[:, :1728]), 0)
    one = by_core(side, one, swap(one), 0)
    grad_one = one.reshape(2, 16, 2, 128).transpose(0, 2, 1, 3).reshape(C1, 128)[:, :108]
    return grad_one, grad_two


def body(density, weight_one, weight_two, feature_cot):
    taps = jnp.asarray(window_taps(), BF16)
    side = lax.axis_index("core")
    with jax.named_scope("strip"):
        own, other = strip_parts(density, side)
    with jax.named_scope("weights"):
        fine_weight = jnp.einsum(
            "ok,srk->sor", jnp.pad(weight_one, ((0, 0), (0, 20))), taps, preferred_element_type=F32
        ).astype(BF16).reshape(512, 256)
        forward, backward = coarse_weights(weight_two)
        cot = feature_cot.transpose(1, 0, 2).reshape(64, CELLS)
    features, terms = levels(
        side.astype(jnp.int32).reshape(1), own, other, fine_weight, forward, backward, cot, taps
    )
    features = features.reshape(2, 32, CELLS).transpose(1, 0, 2)
    with jax.named_scope("sums"):
        grad_one, grad_two = sum_grads(terms, side)
    return features, grad_one, grad_two


def solution(mesh):
    fine_mesh = Mesh(mesh.devices.reshape(4, 2, 2, 4, 2), CHIP)
    gx, gy = ("x", "zh"), ("zl", "y", "core")
    return jax.shard_map(
        body,
        mesh=fine_mesh,
        in_specs=(P(None, gx, gy), P(), P(gx, None), P(gx, gy, None)),
        out_specs=(P(gx, gy, None), P(), P(gx, None)),
        check_vma=False,
    )
```

```python
import jax
import jax.numpy as jnp
import numpy as np
from jax import lax
from jax.experimental import pallas as pl
from jax.experimental.pallas import tpu as pltpu
from jax.sharding import Mesh, PartitionSpec as P

C0 = 4
C1 = 64
Z = 64
HZ = 32
CELLS = 4096
ROWS = 4
TILE = 512
WIDE = 2048
SENT = 2304
CHIP = ("x", "zh", "zl", "y", "core")
F32 = jnp.float32
BF16 = jnp.bfloat16


def split_depth():
    sort = np.zeros((1024, 1024), np.float32)
    for y in range(16):
        for z in range(Z):
            sort[y * Z + z, ((y % 2) * 2 + z % 2) * 256 + (y // 2) * HZ + z // 2] = 1
    return sort


def window_taps():
    place = {(1, 1): 0, (0, 0): 1, (0, 1): 2, (1, 0): 3}
    taps = np.zeros((8, 256, 128), np.float32)
    for cell in range(8):
        a, b, c = cell // 4, cell // 2 % 2, cell % 2
        for x in range(4):
            for y_key, y in place.items():
                for z_key, z in place.items():
                    dx, dy, dz = x - a, y - b, z - c
                    if min(dx, dy, dz) < 0 or max(dx, dy, dz) > 2:
                        continue
                    row = x * 64 + y_key[0] * 32 + z_key[0] * 16 + y_key[1] * 8 + z_key[1] * 4
                    for i in range(C0):
                        taps[cell, row + i, (9 * dx + 3 * dy + dz) * C0 + i] = 1
    return taps


def depth_of(shape):
    return lax.broadcasted_iota(jnp.int32, shape, 1) % HZ


def move(values, step):
    return pltpu.roll(values, step % values.shape[1], 1)


def from_below(values, depth):
    return jnp.where(depth != 0, move(values, 1), 0.0)


def from_above(values, depth):
    return jnp.where(depth != HZ - 1, move(values, -1), 0.0)


def place_windows(cells, windows_ref, at):
    depth = depth_of((8, CELLS))
    low = lax.broadcasted_iota(jnp.int32, (8, CELLS), 0) < 4
    cells = cells.astype(F32)
    even, odd = cells[:8], cells[8:]
    for shifted, (top, bottom) in enumerate(((even, odd), (move(even, -HZ), move(odd, HZ)))):
        here = pl.multiple_of(at + 32 * shifted, 32)
        windows_ref[pl.ds(here, 16), :] = jnp.concatenate([top, bottom], axis=0).astype(BF16)
        moved = [
            jnp.where(low, from_above(half, depth), from_below(half, depth))
            for half in (top, bottom)
        ]
        windows_ref[pl.ds(here + 16, 16), :] = jnp.concatenate(moved, axis=0).astype(BF16)


def levels_kernel(
    side_ref, own_ref, other_ref, fine_ref, forward_ref, backward_ref, cot_ref, taps_ref,
    feature_ref, keep_ref, send_ref,
    windows_ref, slope_ref, pooled_ref, wide_ref, moved_ref, back_ref, sum_ref,
):
    side = side_ref[0]

    for x in range(10):
        rows = pl.ds(pl.multiple_of(16 * (x + 4 * side), 16), 16)
        cells = []
        for chip in range(8):
            mine, theirs = own_ref[chip, rows, :], other_ref[chip, rows, :]
            cells.append(jnp.where(side == 0, mine, theirs))
            cells.append(jnp.where(side == 0, theirs, mine))
        place_windows(jnp.concatenate(cells, axis=1), windows_ref, 64 * x)

    for step in range(ROWS * CELLS // WIDE):
        row, tile = step // (CELLS // WIDE), step % (CELLS // WIDE)
        lanes = slice(tile * WIDE, tile * WIDE + WIDE)
        window = windows_ref[row * 128 : row * 128 + 256, lanes]
        pre = jnp.dot(fine_ref[...], window, preferred_element_type=F32)
        total = None
        for cell in range(8):
            value = pre[C1 * cell : C1 * cell + C1].astype(BF16)
            bent = jnp.tanh(value)
            gate = bent + 0.65 / 0.35
            act = value * gate
            slope_ref[row * 8 + cell, :, lanes] = gate + value * (1.0 - bent * bent)
            total = act if total is None else total + act
        pooled_ref[row * C1 : row * C1 + C1, lanes] = (
            total.astype(F32) * (0.125 * 0.35)
        ).astype(BF16)

    for tile in range(CELLS // TILE):
        lanes = slice(tile * TILE, tile * TILE + TILE)
        wide_ref[:, lanes] = jnp.dot(forward_ref[...], pooled_ref[:, lanes], preferred_element_type=F32)
    depth = depth_of((16, CELLS))
    for block in range(4):
        def term(dy, dz):
            at = 64 * (3 * dy + dz) + 16 * block
            return wide_ref[at : at + 16, :]

        def column(dz):
            return term(1, dz) + move(term(0, dz), HZ) + move(term(2, dz), -HZ)

        pre = column(1) + from_below(column(0), depth) + from_above(column(2), depth)
        rows = slice(16 * block, 16 * block + 16)
        bent = jnp.tanh(pre)
        gate = 0.65 + 0.35 * bent
        feature_ref[rows, :] = (pre * gate).astype(BF16)
        slope = gate + 0.35 * pre * (1.0 - bent * bent)
        grads = (cot_ref[rows, :].astype(F32) * slope).astype(BF16).astype(F32)
        for dy in range(3):
            here = grads if dy == 1 else move(grads, HZ * (dy - 1))
            for dz in range(3):
                there = here if dz == 1 else (from_above if dz == 0 else from_below)(here, depth)
                at = 64 * (3 * dy + dz) + 16 * block
                moved_ref[at : at + 16, :] = there.astype(BF16)
    for tile in range(CELLS // TILE):
        lanes = slice(tile * TILE, tile * TILE + TILE)
        back_ref[:, lanes] = jnp.dot(
            backward_ref[...], moved_ref[:, lanes], preferred_element_type=F32
        ).astype(BF16)
    grad = lax.dot_general(
        moved_ref[...], pooled_ref[...], (((1,), (1,)), ((), ())), preferred_element_type=F32
    )
    for tap in range(9):
        both = grad[64 * tap : 64 * tap + 32, :192] + grad[64 * tap + 32 : 64 * tap + 64, 64:]
        keep = jnp.where(side == 0, both[:16], both[16:])
        send = jnp.where(side == 0, both[16:], both[:16])
        for dx in range(3):
            at = dx * 576 + tap * 64
            keep_ref[:, at : at + 64] = keep[:, 64 * dx : 64 * dx + 64]
            send_ref[:, at : at + 64] = send[:, 64 * dx : 64 * dx + 64]
    keep_ref[:, 1728:1792] = jnp.zeros((16, 64), F32)
    send_ref[:, 1728:1792] = jnp.zeros((16, 64), F32)

    sum_ref[...] = jnp.zeros_like(sum_ref)

    def back_step(row, _):
        window = windows_ref[pl.ds(pl.multiple_of(row * 128, 128), 256), :]
        back = back_ref[pl.ds(pl.multiple_of(row * C1, C1), C1), :]
        grads = jnp.concatenate([slope_ref[row * 8 + cell] * back for cell in range(8)], axis=0)
        sum_ref[...] += lax.dot_general(
            grads, window, (((1,), (1,)), ((), ())), preferred_element_type=F32
        )
        return 0

    lax.fori_loop(0, ROWS, back_step, 0)
    total = jnp.zeros((C1, 128), F32)
    for cell in range(8):
        whole = sum_ref[C1 * cell : C1 * cell + C1, :]
        high = whole.astype(BF16)
        low = (whole - high.astype(F32)).astype(BF16)
        total += jnp.dot(high, taps_ref[cell], preferred_element_type=F32)
        total += jnp.dot(low, taps_ref[cell], preferred_element_type=F32)
    total = total * (0.125 * 0.35)
    for part in range(4):
        lanes = slice(1792 + 128 * part, 1920 + 128 * part)
        keep_ref[:, lanes] = total[16 * part : 16 * part + 16]
        send_ref[:, lanes] = total[16 * part : 16 * part + 16]


def levels(side, own, other, fine, forward, backward, cot, taps):
    whole = pl.BlockSpec(memory_space=pltpu.VMEM)
    return pl.pallas_call(
        levels_kernel,
        in_specs=[pl.BlockSpec(memory_space=pltpu.SMEM)]
        + [whole] * 7,
        out_specs=[whole] * 3,
        out_shape=[
            jax.ShapeDtypeStruct((64, CELLS), BF16),
            jax.ShapeDtypeStruct((16, SENT), F32),
            jax.ShapeDtypeStruct((16, SENT), F32),
        ],
        scratch_shapes=[
            pltpu.VMEM((640, CELLS), BF16),
            pltpu.VMEM((32, C1, CELLS), BF16),
            pltpu.VMEM((ROWS * C1, CELLS), BF16),
            pltpu.VMEM((576, CELLS), F32),
            pltpu.VMEM((576, CELLS), BF16),
            pltpu.VMEM((ROWS * C1, CELLS), BF16),
            pltpu.VMEM((512, 256), F32),
        ],
        compiler_params=pltpu.CompilerParams(vmem_limit_bytes=48 << 20),
        name="levels",
    )(side, own, other, fine, forward, backward, cot, taps)


def swap(values):
    return lax.ppermute(values, "core", [(0, 1), (1, 0)])


def by_core(side, mine, other, dim):
    return jnp.where(
        side == 0, jnp.concatenate([mine, other], dim), jnp.concatenate([other, mine], dim)
    )


def strip_parts(density):
    sort = jnp.asarray(split_depth(), BF16)
    sorted_cells = jnp.dot(density.reshape(32, 1024), sort, preferred_element_type=F32).astype(BF16)
    block = sorted_cells.reshape(C0, 8, 4, 256).transpose(1, 2, 0, 3).reshape(128, 256)
    column = lax.all_to_all(jnp.broadcast_to(block[None], (8, 128, 256)), ("x", "zh"), 0, 0)
    strips = jnp.concatenate(
        [jnp.roll(column[:, 80:], 1, 0), column, jnp.roll(column[:, :48], -1, 0)], axis=1
    )
    return lax.all_to_all(strips, ("zl", "y"), 0, 0)


def coarse_weights(weight_two):
    taps = weight_two.reshape(32, 3, 9, C1)
    both = jnp.stack([jnp.pad(taps, ((0, 0), (r, 1 - r), (0, 0), (0, 0))) for r in range(2)])
    forward = both.transpose(3, 0, 1, 2, 4).reshape(576, 256)
    return forward, forward.T


def sum_near(keep, send, features):
    mine = (keep + swap(send)).astype(BF16)
    copies = jnp.broadcast_to(mine[None], (8, 16, SENT))
    terms, features = lax.optimization_barrier(
        (lax.all_to_all(copies, ("zl", "y"), 0, 0), features)
    )
    return terms.astype(F32).sum(0), features


def sum_far(copies):
    one = lax.all_to_all(copies, ("x", "zh"), 0, 0).astype(F32).sum(0)
    return one.reshape(16, 4, 128).transpose(1, 0, 2).reshape(C1, 128)[:, :108]


def body(density, weight_one, weight_two, feature_cot):
    taps = jnp.asarray(window_taps(), BF16)
    side = lax.axis_index("core")
    with jax.named_scope("strip"):
        own = strip_parts(density)
    with jax.named_scope("weights"):
        fine_weight = jnp.einsum(
            "ok,srk->sor", jnp.pad(weight_one, ((0, 0), (0, 20))), taps, preferred_element_type=F32
        ).astype(BF16).reshape(512, 256)
        forward, backward = coarse_weights(weight_two)
        cot = feature_cot.transpose(1, 0, 2).reshape(64, CELLS)
    own, fine_weight, forward, backward, cot = lax.optimization_barrier(
        (own, fine_weight, forward, backward, cot)
    )
    features, keep, send = levels(
        side.astype(jnp.int32).reshape(1), own, swap(own), fine_weight, forward, backward, cot, taps
    )
    features = features.reshape(2, 32, CELLS).transpose(1, 0, 2)
    with jax.named_scope("sums"):
        summed, features = sum_near(keep, send, features)
        copies = jnp.broadcast_to(summed[None, :, 1792:].astype(BF16), (8, 16, 512))
        grad_one = sum_far(copies)
        grad_two = by_core(side, summed[:, :1728], swap(summed[:, :1728]), 0)
    return features, grad_one, grad_two


def solution(mesh):
    fine_mesh = Mesh(mesh.devices.reshape(4, 2, 2, 4, 2), CHIP)
    gx, gy = ("x", "zh"), ("zl", "y", "core")
    return jax.shard_map(
        body,
        mesh=fine_mesh,
        in_specs=(P(None, gx, gy), P(), P(gx, None), P(gx, gy, None)),
        out_specs=(P(gx, gy, None), P(), P(gx, None)),
        check_vma=False,
    )
```

```python
import jax
import jax.numpy as jnp
import numpy as np
from jax import lax
from jax.experimental import pallas as pl
from jax.experimental.pallas import tpu as pltpu
from jax.sharding import Mesh, PartitionSpec as P

C0 = 4
C1 = 64
Z = 64
HZ = 32
CELLS = 4096
ROWS = 4
TILE = 512
WIDE = 2048
CHIP = ("x", "zh", "zl", "y", "core")
F32 = jnp.float32
BF16 = jnp.bfloat16


def split_depth():
    sort = np.zeros((1024, 1024), np.float32)
    for y in range(16):
        for z in range(Z):
            sort[y * Z + z, ((y % 2) * 2 + z % 2) * 256 + (y // 2) * HZ + z // 2] = 1
    return sort


def window_taps():
    place = {(1, 1): 0, (0, 0): 1, (0, 1): 2, (1, 0): 3}
    taps = np.zeros((8, 256, 128), np.float32)
    for cell in range(8):
        a, b, c = cell // 4, cell // 2 % 2, cell % 2
        for x in range(4):
            for y_key, y in place.items():
                for z_key, z in place.items():
                    dx, dy, dz = x - a, y - b, z - c
                    if min(dx, dy, dz) < 0 or max(dx, dy, dz) > 2:
                        continue
                    row = x * 64 + y_key[0] * 32 + z_key[0] * 16 + y_key[1] * 8 + z_key[1] * 4
                    for i in range(C0):
                        taps[cell, row + i, (9 * dx + 3 * dy + dz) * C0 + i] = 1
    return taps


def depth_of(shape):
    return lax.broadcasted_iota(jnp.int32, shape, 1) % HZ


def move(values, step):
    return pltpu.roll(values, step % values.shape[1], 1)


def from_below(values, depth):
    return jnp.where(depth != 0, move(values, 1), 0.0)


def from_above(values, depth):
    return jnp.where(depth != HZ - 1, move(values, -1), 0.0)


def place_windows(cells, windows_ref, at):
    depth = depth_of((8, CELLS))
    low = lax.broadcasted_iota(jnp.int32, (8, CELLS), 0) < 4
    cells = cells.astype(F32)
    even, odd = cells[:8], cells[8:]
    for shifted, (top, bottom) in enumerate(((even, odd), (move(even, -HZ), move(odd, HZ)))):
        here = pl.multiple_of(at + 32 * shifted, 32)
        windows_ref[pl.ds(here, 16), :] = jnp.concatenate([top, bottom], axis=0).astype(BF16)
        moved = [
            jnp.where(low, from_above(half, depth), from_below(half, depth))
            for half in (top, bottom)
        ]
        windows_ref[pl.ds(here + 16, 16), :] = jnp.concatenate(moved, axis=0).astype(BF16)


def levels_kernel(
    side_ref, own_ref, other_ref, fine_ref, forward_ref, backward_ref, cot_ref, taps_ref,
    feature_ref, keep_ref, send_ref, keep_one_ref, send_one_ref,
    windows_ref, slope_ref, pooled_ref, wide_ref, moved_ref, back_ref, sum_ref,
):
    side = side_ref[0]

    for x in range(10):
        rows = pl.ds(pl.multiple_of(16 * (x + 4 * side), 16), 16)
        cells = []
        for chip in range(8):
            mine, theirs = own_ref[chip, rows, :], other_ref[chip, rows, :]
            cells.append(jnp.where(side == 0, mine, theirs))
            cells.append(jnp.where(side == 0, theirs, mine))
        place_windows(jnp.concatenate(cells, axis=1), windows_ref, 64 * x)

    for step in range(ROWS * CELLS // WIDE):
        row, tile = step // (CELLS // WIDE), step % (CELLS // WIDE)
        lanes = slice(tile * WIDE, tile * WIDE + WIDE)
        window = windows_ref[row * 128 : row * 128 + 256, lanes]
        pre = jnp.dot(fine_ref[...], window, preferred_element_type=F32)
        total = None
        for cell in range(8):
            value = pre[C1 * cell : C1 * cell + C1].astype(BF16)
            bent = jnp.tanh(value)
            gate = bent + 0.65 / 0.35
            act = value * gate
            slope_ref[row * 8 + cell, :, lanes] = gate + value * (1.0 - bent * bent)
            total = act if total is None else total + act
        pooled_ref[row * C1 : row * C1 + C1, lanes] = (
            total.astype(F32) * (0.125 * 0.35)
        ).astype(BF16)

    for tile in range(CELLS // TILE):
        lanes = slice(tile * TILE, tile * TILE + TILE)
        wide_ref[:, lanes] = jnp.dot(forward_ref[...], pooled_ref[:, lanes], preferred_element_type=F32)
    depth = depth_of((16, CELLS))
    for block in range(4):
        def term(dy, dz):
            at = 64 * (3 * dy + dz) + 16 * block
            return wide_ref[at : at + 16, :]

        def column(dz):
            return term(1, dz) + move(term(0, dz), HZ) + move(term(2, dz), -HZ)

        pre = column(1) + from_below(column(0), depth) + from_above(column(2), depth)
        rows = slice(16 * block, 16 * block + 16)
        bent = jnp.tanh(pre)
        gate = 0.65 + 0.35 * bent
        feature_ref[rows, :] = (pre * gate).astype(BF16)
        slope = gate + 0.35 * pre * (1.0 - bent * bent)
        grads = (cot_ref[rows, :].astype(F32) * slope).astype(BF16).astype(F32)
        for dy in range(3):
            here = grads if dy == 1 else move(grads, HZ * (dy - 1))
            for dz in range(3):
                there = here if dz == 1 else (from_above if dz == 0 else from_below)(here, depth)
                at = 64 * (3 * dy + dz) + 16 * block
                moved_ref[at : at + 16, :] = there.astype(BF16)
    for tile in range(CELLS // TILE):
        lanes = slice(tile * TILE, tile * TILE + TILE)
        back_ref[:, lanes] = jnp.dot(
            backward_ref[...], moved_ref[:, lanes], preferred_element_type=F32
        ).astype(BF16)
    grad = lax.dot_general(
        moved_ref[...], pooled_ref[...], (((1,), (1,)), ((), ())), preferred_element_type=F32
    )
    for tap in range(9):
        both = grad[64 * tap : 64 * tap + 32, :192] + grad[64 * tap + 32 : 64 * tap + 64, 64:]
        keep = jnp.where(side == 0, both[:16], both[16:])
        send = jnp.where(side == 0, both[16:], both[:16])
        for dx in range(3):
            at = dx * 576 + tap * 64
            keep_ref[:, at : at + 64] = keep[:, 64 * dx : 64 * dx + 64]
            send_ref[:, at : at + 64] = send[:, 64 * dx : 64 * dx + 64]
    sum_ref[...] = jnp.zeros_like(sum_ref)

    def back_step(row, _):
        window = windows_ref[pl.ds(pl.multiple_of(row * 128, 128), 256), :]
        back = back_ref[pl.ds(pl.multiple_of(row * C1, C1), C1), :]
        grads = jnp.concatenate([slope_ref[row * 8 + cell] * back for cell in range(8)], axis=0)
        sum_ref[...] += lax.dot_general(
            grads, window, (((1,), (1,)), ((), ())), preferred_element_type=F32
        )
        return 0

    lax.fori_loop(0, ROWS, back_step, 0)
    total = jnp.zeros((C1, 128), F32)
    for cell in range(8):
        whole = sum_ref[C1 * cell : C1 * cell + C1, :]
        high = whole.astype(BF16)
        low = (whole - high.astype(F32)).astype(BF16)
        total += jnp.dot(high, taps_ref[cell], preferred_element_type=F32)
        total += jnp.dot(low, taps_ref[cell], preferred_element_type=F32)
    total = total * (0.125 * 0.35)
    keep_one_ref[...] = jnp.where(side == 0, total[:32], total[32:])
    send_one_ref[...] = jnp.where(side == 0, total[32:], total[:32])


def levels(side, own, other, fine, forward, backward, cot, taps):
    whole = pl.BlockSpec(memory_space=pltpu.VMEM)
    return pl.pallas_call(
        levels_kernel,
        in_specs=[pl.BlockSpec(memory_space=pltpu.SMEM)]
        + [whole] * 7,
        out_specs=[whole] * 5,
        out_shape=[
            jax.ShapeDtypeStruct((64, CELLS), BF16),
            jax.ShapeDtypeStruct((16, 1728), F32),
            jax.ShapeDtypeStruct((16, 1728), F32),
            jax.ShapeDtypeStruct((32, 128), F32),
            jax.ShapeDtypeStruct((32, 128), F32),
        ],
        scratch_shapes=[
            pltpu.VMEM((640, CELLS), BF16),
            pltpu.VMEM((32, C1, CELLS), BF16),
            pltpu.VMEM((ROWS * C1, CELLS), BF16),
            pltpu.VMEM((576, CELLS), F32),
            pltpu.VMEM((576, CELLS), BF16),
            pltpu.VMEM((ROWS * C1, CELLS), BF16),
            pltpu.VMEM((512, 256), F32),
        ],
        compiler_params=pltpu.CompilerParams(vmem_limit_bytes=48 << 20),
        name="levels",
    )(side, own, other, fine, forward, backward, cot, taps)


def swap(values):
    return lax.ppermute(values, "core", [(0, 1), (1, 0)])


def by_core(side, mine, other, dim):
    return jnp.where(
        side == 0, jnp.concatenate([mine, other], dim), jnp.concatenate([other, mine], dim)
    )


def strip_parts(density):
    sort = jnp.asarray(split_depth(), BF16)
    sorted_cells = jnp.dot(density.reshape(32, 1024), sort, preferred_element_type=F32).astype(BF16)
    block = sorted_cells.reshape(C0, 8, 4, 256).transpose(1, 2, 0, 3).reshape(128, 256)
    column = lax.all_to_all(jnp.broadcast_to(block[None], (8, 128, 256)), ("x", "zh"), 0, 0)
    strips = jnp.concatenate(
        [jnp.roll(column[:, 80:], 1, 0), column, jnp.roll(column[:, :48], -1, 0)], axis=1
    )
    return lax.all_to_all(strips, ("zl", "y"), 0, 0)


def coarse_weights(weight_two):
    taps = weight_two.reshape(32, 3, 9, C1)
    both = jnp.stack([jnp.pad(taps, ((0, 0), (r, 1 - r), (0, 0), (0, 0))) for r in range(2)])
    forward = both.transpose(3, 0, 1, 2, 4).reshape(576, 256)
    return forward, forward.T


def ring(count, step):
    return [(i, (i + step) % count) for i in range(count)]


def sum_one(keep, send, features, side):
    mine = (keep + swap(send)).astype(BF16)
    copies = jnp.broadcast_to(mine[None], (64, 32, 128))
    terms = lax.all_to_all(copies, CHIP[:4], 0, 0)
    terms, features = lax.optimization_barrier((terms, features))
    half = terms.astype(F32).sum(0)
    return by_core(side, half, swap(half), 0)[:, :108], features


def sum_two(keep, send, side):
    mine = (keep + swap(send)).astype(BF16)
    mine = (mine.astype(F32) + lax.ppermute(mine, "zl", ring(2, 1)).astype(F32)).astype(BF16)
    terms = [lax.ppermute(mine, "y", ring(4, step)).astype(F32) for step in range(1, 4)]
    half = mine.astype(F32) + terms[0] + terms[1] + terms[2]
    return by_core(side, half, swap(half), 0)


def body(density, weight_one, weight_two, feature_cot):
    taps = jnp.asarray(window_taps(), BF16)
    side = lax.axis_index("core")
    with jax.named_scope("strip"):
        own = strip_parts(density)
    with jax.named_scope("weights"):
        fine_weight = jnp.einsum(
            "ok,srk->sor", jnp.pad(weight_one, ((0, 0), (0, 20))), taps, preferred_element_type=F32
        ).astype(BF16).reshape(512, 256)
        forward, backward = coarse_weights(weight_two)
        cot = feature_cot.transpose(1, 0, 2).reshape(64, CELLS)
    own, fine_weight, forward, backward, cot = lax.optimization_barrier(
        (own, fine_weight, forward, backward, cot)
    )
    features, keep, send, keep_one, send_one = levels(
        side.astype(jnp.int32).reshape(1), own, swap(own), fine_weight, forward, backward, cot, taps
    )
    features = features.reshape(2, 32, CELLS).transpose(1, 0, 2)
    with jax.named_scope("sums"):
        grad_one, features = sum_one(keep_one, send_one, features, side)
        grad_two = sum_two(keep, send, side)
    return features, grad_one, grad_two


def solution(mesh):
    fine_mesh = Mesh(mesh.devices.reshape(4, 2, 2, 4, 2), CHIP)
    gx, gy = ("x", "zh"), ("zl", "y", "core")
    return jax.shard_map(
        body,
        mesh=fine_mesh,
        in_specs=(P(None, gx, gy), P(), P(gx, None), P(gx, gy, None)),
        out_specs=(P(gx, gy, None), P(), P(gx, None)),
        check_vma=False,
    )
```

```python
import jax
import jax.numpy as jnp
import numpy as np
from jax import lax
from jax.experimental import pallas as pl
from jax.experimental.pallas import tpu as pltpu
from jax.sharding import Mesh, PartitionSpec as P

C0 = 4
C1 = 64
Z = 64
HZ = 32
CELLS = 4096
ROWS = 4
TILE = 512
WIDE = 2048
CHIP = ("x", "zh", "zl", "y", "core")
F32 = jnp.float32
BF16 = jnp.bfloat16


def iota(size, axis):
    return lax.broadcasted_iota(jnp.int32, (size, size), axis)


def sort_kernel(density_ref, copies_ref):
    cells = jnp.concatenate([density_ref[i].astype(F32) for i in range(C0)], axis=0)
    cells = jnp.concatenate([cells[:, :512], cells[:, 512:]], axis=0).astype(BF16)
    y, z = iota(512, 0) // Z, iota(512, 0) % Z
    lane = ((y % 2) * 2 + z % 2) * 128 + (y // 2) * HZ + z // 2
    lanes = jnp.where(lane == iota(512, 1), 1.0, 0.0).astype(BF16)
    sorted_cells = jnp.dot(cells, lanes, preferred_element_type=F32)
    halves = [
        jnp.concatenate(
            [sorted_cells[32 * h : 32 * h + 32, 128 * p : 128 * p + 128] for p in range(4)], axis=0
        )
        for h in range(2)
    ]
    row = iota(128, 0)
    source = row // C0 % 4 * 32 + row % C0 * 8 + row // 16
    rows = jnp.where(source == iota(128, 1), 1.0, 0.0).astype(BF16)
    block = jnp.dot(
        rows, jnp.concatenate(halves, axis=1).astype(BF16), preferred_element_type=F32
    ).astype(BF16)
    for copy in range(8):
        copies_ref[copy] = block


def window_taps():
    place = {(1, 1): 0, (0, 0): 1, (0, 1): 2, (1, 0): 3}
    taps = np.zeros((8, 256, 128), np.float32)
    for cell in range(8):
        a, b, c = cell // 4, cell // 2 % 2, cell % 2
        for x in range(4):
            for y_key, y in place.items():
                for z_key, z in place.items():
                    dx, dy, dz = x - a, y - b, z - c
                    if min(dx, dy, dz) < 0 or max(dx, dy, dz) > 2:
                        continue
                    row = x * 64 + y_key[0] * 32 + z_key[0] * 16 + y_key[1] * 8 + z_key[1] * 4
                    for i in range(C0):
                        taps[cell, row + i, (9 * dx + 3 * dy + dz) * C0 + i] = 1
    return taps


def depth_of(shape):
    return lax.broadcasted_iota(jnp.int32, shape, 1) % HZ


def move(values, step):
    return pltpu.roll(values, step % values.shape[1], 1)


def from_below(values, depth):
    return jnp.where(depth != 0, move(values, 1), 0.0)


def from_above(values, depth):
    return jnp.where(depth != HZ - 1, move(values, -1), 0.0)


def place_windows(cells, windows_ref, at):
    depth = depth_of((8, CELLS))
    low = lax.broadcasted_iota(jnp.int32, (8, CELLS), 0) < 4
    cells = cells.astype(F32)
    even, odd = cells[:8], cells[8:]
    for shifted, (top, bottom) in enumerate(((even, odd), (move(even, -HZ), move(odd, HZ)))):
        here = pl.multiple_of(at + 32 * shifted, 32)
        windows_ref[pl.ds(here, 16), :] = jnp.concatenate([top, bottom], axis=0).astype(BF16)
        moved = [
            jnp.where(low, from_above(half, depth), from_below(half, depth))
            for half in (top, bottom)
        ]
        windows_ref[pl.ds(here + 16, 16), :] = jnp.concatenate(moved, axis=0).astype(BF16)


def levels_kernel(
    side_ref, own_ref, other_ref, fine_ref, forward_ref, backward_ref, cot_ref, taps_ref,
    feature_ref, keep_ref, send_ref, keep_one_ref, send_one_ref,
    windows_ref, slope_ref, pooled_ref, wide_ref, moved_ref, back_ref, sum_ref,
):
    side = side_ref[0]

    for x in range(10):
        rows = pl.ds(pl.multiple_of(16 * (x + 4 * side), 16), 16)
        cells = []
        for chip in range(8):
            mine, theirs = own_ref[chip, rows, :], other_ref[chip, rows, :]
            cells.append(jnp.where(side == 0, mine, theirs))
            cells.append(jnp.where(side == 0, theirs, mine))
        place_windows(jnp.concatenate(cells, axis=1), windows_ref, 64 * x)

    for step in range(ROWS * CELLS // WIDE):
        row, tile = step // (CELLS // WIDE), step % (CELLS // WIDE)
        lanes = slice(tile * WIDE, tile * WIDE + WIDE)
        window = windows_ref[row * 128 : row * 128 + 256, lanes]
        pre = jnp.dot(fine_ref[...], window, preferred_element_type=F32)
        total = None
        for cell in range(8):
            value = pre[C1 * cell : C1 * cell + C1].astype(BF16)
            bent = jnp.tanh(value)
            gate = bent + 0.65 / 0.35
            act = value * gate
            slope_ref[row * 8 + cell, :, lanes] = gate + value * (1.0 - bent * bent)
            total = act if total is None else total + act
        pooled_ref[row * C1 : row * C1 + C1, lanes] = (
            total.astype(F32) * (0.125 * 0.35)
        ).astype(BF16)

    for tile in range(CELLS // TILE):
        lanes = slice(tile * TILE, tile * TILE + TILE)
        wide_ref[:, lanes] = jnp.dot(forward_ref[...], pooled_ref[:, lanes], preferred_element_type=F32)
    depth = depth_of((16, CELLS))
    for block in range(4):
        def term(dy, dz):
            at = 64 * (3 * dy + dz) + 16 * block
            return wide_ref[at : at + 16, :]

        def column(dz):
            return term(1, dz) + move(term(0, dz), HZ) + move(term(2, dz), -HZ)

        pre = column(1) + from_below(column(0), depth) + from_above(column(2), depth)
        rows = slice(16 * block, 16 * block + 16)
        bent = jnp.tanh(pre)
        gate = 0.65 + 0.35 * bent
        feature_ref[rows, :] = (pre * gate).astype(BF16)
        slope = gate + 0.35 * pre * (1.0 - bent * bent)
        grads = (cot_ref[rows, :].astype(F32) * slope).astype(BF16).astype(F32)
        for dy in range(3):
            here = grads if dy == 1 else move(grads, HZ * (dy - 1))
            for dz in range(3):
                there = here if dz == 1 else (from_above if dz == 0 else from_below)(here, depth)
                at = 64 * (3 * dy + dz) + 16 * block
                moved_ref[at : at + 16, :] = there.astype(BF16)
    for tile in range(CELLS // TILE):
        lanes = slice(tile * TILE, tile * TILE + TILE)
        back_ref[:, lanes] = jnp.dot(
            backward_ref[...], moved_ref[:, lanes], preferred_element_type=F32
        ).astype(BF16)
    grad = lax.dot_general(
        moved_ref[...], pooled_ref[...], (((1,), (1,)), ((), ())), preferred_element_type=F32
    )
    for tap in range(9):
        both = grad[64 * tap : 64 * tap + 32, :192] + grad[64 * tap + 32 : 64 * tap + 64, 64:]
        keep = jnp.where(side == 0, both[:16], both[16:])
        send = jnp.where(side == 0, both[16:], both[:16])
        for dx in range(3):
            at = dx * 576 + tap * 64
            keep_ref[:, at : at + 64] = keep[:, 64 * dx : 64 * dx + 64]
            send_ref[:, at : at + 64] = send[:, 64 * dx : 64 * dx + 64]
    sum_ref[...] = jnp.zeros_like(sum_ref)

    def back_step(row, _):
        window = windows_ref[pl.ds(pl.multiple_of(row * 128, 128), 256), :]
        back = back_ref[pl.ds(pl.multiple_of(row * C1, C1), C1), :]
        grads = jnp.concatenate([slope_ref[row * 8 + cell] * back for cell in range(8)], axis=0)
        sum_ref[...] += lax.dot_general(
            grads, window, (((1,), (1,)), ((), ())), preferred_element_type=F32
        )
        return 0

    lax.fori_loop(0, ROWS, back_step, 0, unroll=2)
    total = jnp.zeros((C1, 128), F32)
    for cell in range(8):
        whole = sum_ref[C1 * cell : C1 * cell + C1, :]
        high = whole.astype(BF16)
        low = (whole - high.astype(F32)).astype(BF16)
        total += jnp.dot(high, taps_ref[cell], preferred_element_type=F32)
        total += jnp.dot(low, taps_ref[cell], preferred_element_type=F32)
    total = total * (0.125 * 0.35)
    keep_one_ref[...] = jnp.where(side == 0, total[:32], total[32:])
    send_one_ref[...] = jnp.where(side == 0, total[32:], total[:32])


def levels(side, own, other, fine, forward, backward, cot, taps):
    whole = pl.BlockSpec(memory_space=pltpu.VMEM)
    return pl.pallas_call(
        levels_kernel,
        in_specs=[pl.BlockSpec(memory_space=pltpu.SMEM)]
        + [whole] * 7,
        out_specs=[whole] * 5,
        out_shape=[
            jax.ShapeDtypeStruct((64, CELLS), BF16),
            jax.ShapeDtypeStruct((16, 1728), F32),
            jax.ShapeDtypeStruct((16, 1728), F32),
            jax.ShapeDtypeStruct((32, 128), F32),
            jax.ShapeDtypeStruct((32, 128), F32),
        ],
        scratch_shapes=[
            pltpu.VMEM((640, CELLS), BF16),
            pltpu.VMEM((32, C1, CELLS), BF16),
            pltpu.VMEM((ROWS * C1, CELLS), BF16),
            pltpu.VMEM((576, CELLS), F32),
            pltpu.VMEM((576, CELLS), BF16),
            pltpu.VMEM((ROWS * C1, CELLS), BF16),
            pltpu.VMEM((512, 256), F32),
        ],
        compiler_params=pltpu.CompilerParams(vmem_limit_bytes=48 << 20),
        name="levels",
    )(side, own, other, fine, forward, backward, cot, taps)


def swap(values):
    return lax.ppermute(values, "core", [(0, 1), (1, 0)])


def by_core(side, mine, other, dim):
    return jnp.where(
        side == 0, jnp.concatenate([mine, other], dim), jnp.concatenate([other, mine], dim)
    )


def strip_parts(density):
    whole = pl.BlockSpec(memory_space=pltpu.VMEM)
    copies = pl.pallas_call(
        sort_kernel,
        in_specs=[whole],
        out_specs=whole,
        out_shape=jax.ShapeDtypeStruct((8, 128, 256), BF16),
        compiler_params=pltpu.CompilerParams(vmem_limit_bytes=8 << 20),
        name="sort_block",
    )(density)
    column = lax.all_to_all(copies, ("x", "zh"), 0, 0)
    strips = jnp.concatenate(
        [jnp.roll(column[:, 80:], 1, 0), column, jnp.roll(column[:, :48], -1, 0)], axis=1
    )
    return lax.all_to_all(strips, ("zl", "y"), 0, 0)


def coarse_weights(weight_two):
    taps = weight_two.reshape(32, 3, 9, C1)
    both = jnp.stack([jnp.pad(taps, ((0, 0), (r, 1 - r), (0, 0), (0, 0))) for r in range(2)])
    forward = both.transpose(3, 0, 1, 2, 4).reshape(576, 256)
    return forward, forward.T


def ring(count, step):
    return [(i, (i + step) % count) for i in range(count)]


def sum_one(keep, send, features, side):
    mine = (keep + swap(send)).astype(BF16)
    copies = jnp.broadcast_to(mine[None], (64, 32, 128))
    terms = lax.all_to_all(copies, CHIP[:4], 0, 0)
    terms, features = lax.optimization_barrier((terms, features))
    half = terms.astype(F32).sum(0)
    return by_core(side, half, swap(half), 0)[:, :108], features


def sum_two(keep, send, side):
    mine = (keep + swap(send)).astype(BF16)
    mine = (mine.astype(F32) + lax.ppermute(mine, "zl", ring(2, 1)).astype(F32)).astype(BF16)
    terms = [lax.ppermute(mine, "y", ring(4, step)).astype(F32) for step in range(1, 4)]
    half = mine.astype(F32) + terms[0] + terms[1] + terms[2]
    return by_core(side, half, swap(half), 0)


def body(density, weight_one, weight_two, feature_cot):
    taps = jnp.asarray(window_taps(), BF16)
    side = lax.axis_index("core")
    with jax.named_scope("strip"):
        own = strip_parts(density)
    with jax.named_scope("weights"):
        fine_weight = jnp.einsum(
            "ok,srk->sor", jnp.pad(weight_one, ((0, 0), (0, 20))), taps, preferred_element_type=F32
        ).astype(BF16).reshape(512, 256)
        forward, backward = coarse_weights(weight_two)
        cot = feature_cot.transpose(1, 0, 2).reshape(64, CELLS)
    own, fine_weight, forward, backward, cot = lax.optimization_barrier(
        (own, fine_weight, forward, backward, cot)
    )
    features, keep, send, keep_one, send_one = levels(
        side.astype(jnp.int32).reshape(1), own, swap(own), fine_weight, forward, backward, cot, taps
    )
    features = features.reshape(2, 32, CELLS).transpose(1, 0, 2)
    with jax.named_scope("sums"):
        grad_one, features = sum_one(keep_one, send_one, features, side)
        grad_two = sum_two(keep, send, side)
    return features, grad_one, grad_two


def solution(mesh):
    fine_mesh = Mesh(mesh.devices.reshape(4, 2, 2, 4, 2), CHIP)
    gx, gy = ("x", "zh"), ("zl", "y", "core")
    return jax.shard_map(
        body,
        mesh=fine_mesh,
        in_specs=(P(None, gx, gy), P(), P(gx, None), P(gx, gy, None)),
        out_specs=(P(gx, gy, None), P(), P(gx, None)),
        check_vma=False,
    )
```

```python
import jax
import jax.numpy as jnp
import numpy as np
from jax import lax
from jax.experimental import pallas as pl
from jax.experimental.pallas import tpu as pltpu
from jax.sharding import Mesh, PartitionSpec as P

C0 = 4
C1 = 64
Z = 64
HZ = 32
CELLS = 4096
ROWS = 4
TILE = 512
WIDE = 2048
CHIP = ("x", "zh", "zl", "y", "core")
F32 = jnp.float32
BF16 = jnp.bfloat16


def iota(size, axis):
    return lax.broadcasted_iota(jnp.int32, (size, size), axis)


def sort_kernel(density_ref, copies_ref):
    cells = jnp.concatenate([density_ref[i].astype(F32) for i in range(C0)], axis=0)
    cells = jnp.concatenate([cells[:, :512], cells[:, 512:]], axis=0).astype(BF16)
    y, z = iota(512, 0) // Z, iota(512, 0) % Z
    lane = ((y % 2) * 2 + z % 2) * 128 + (y // 2) * HZ + z // 2
    lanes = jnp.where(lane == iota(512, 1), 1.0, 0.0).astype(BF16)
    sorted_cells = jnp.dot(cells, lanes, preferred_element_type=F32)
    halves = [
        jnp.concatenate(
            [sorted_cells[32 * h : 32 * h + 32, 128 * p : 128 * p + 128] for p in range(4)], axis=0
        )
        for h in range(2)
    ]
    row = iota(128, 0)
    source = row // C0 % 4 * 32 + row % C0 * 8 + row // 16
    rows = jnp.where(source == iota(128, 1), 1.0, 0.0).astype(BF16)
    block = jnp.dot(
        rows, jnp.concatenate(halves, axis=1).astype(BF16), preferred_element_type=F32
    ).astype(BF16)
    for copy in range(8):
        copies_ref[copy] = block


def window_taps():
    place = {(1, 1): 0, (0, 0): 1, (0, 1): 2, (1, 0): 3}
    taps = np.zeros((8, 256, 128), np.float32)
    for cell in range(8):
        a, b, c = cell // 4, cell // 2 % 2, cell % 2
        for x in range(4):
            for y_key, y in place.items():
                for z_key, z in place.items():
                    dx, dy, dz = x - a, y - b, z - c
                    if min(dx, dy, dz) < 0 or max(dx, dy, dz) > 2:
                        continue
                    row = x * 64 + y_key[0] * 32 + z_key[0] * 16 + y_key[1] * 8 + z_key[1] * 4
                    for i in range(C0):
                        taps[cell, row + i, (9 * dx + 3 * dy + dz) * C0 + i] = 1
    return taps


def depth_of(shape):
    return lax.broadcasted_iota(jnp.int32, shape, 1) % HZ


def move(values, step):
    return pltpu.roll(values, step % values.shape[1], 1)


def from_below(values, depth):
    return jnp.where(depth != 0, move(values, 1), 0.0)


def from_above(values, depth):
    return jnp.where(depth != HZ - 1, move(values, -1), 0.0)


def place_windows(cells, windows_ref, at):
    depth = depth_of((8, CELLS))
    low = lax.broadcasted_iota(jnp.int32, (8, CELLS), 0) < 4
    cells = cells.astype(F32)
    even, odd = cells[:8], cells[8:]
    for shifted, (top, bottom) in enumerate(((even, odd), (move(even, -HZ), move(odd, HZ)))):
        here = pl.multiple_of(at + 32 * shifted, 32)
        windows_ref[pl.ds(here, 16), :] = jnp.concatenate([top, bottom], axis=0).astype(BF16)
        moved = [
            jnp.where(low, from_above(half, depth), from_below(half, depth))
            for half in (top, bottom)
        ]
        windows_ref[pl.ds(here + 16, 16), :] = jnp.concatenate(moved, axis=0).astype(BF16)


def levels_kernel(
    side_ref, own_ref, other_ref, fine_ref, forward_ref, backward_ref, cot_ref, taps_ref,
    feature_ref, keep_ref, send_ref, keep_one_ref, send_one_ref,
    windows_ref, slope_ref, pooled_ref, wide_ref, moved_ref, back_ref, sum_ref,
):
    side = side_ref[0]

    for x in range(10):
        rows = pl.ds(pl.multiple_of(16 * (x + 4 * side), 16), 16)
        cells = []
        for chip in range(8):
            mine, theirs = own_ref[chip, rows, :], other_ref[chip, rows, :]
            cells.append(jnp.where(side == 0, mine, theirs))
            cells.append(jnp.where(side == 0, theirs, mine))
        place_windows(jnp.concatenate(cells, axis=1), windows_ref, 64 * x)

    for step in range(ROWS * CELLS // WIDE):
        row, tile = step // (CELLS // WIDE), step % (CELLS // WIDE)
        lanes = slice(tile * WIDE, tile * WIDE + WIDE)
        window = windows_ref[row * 128 : row * 128 + 256, lanes]
        pre = jnp.dot(fine_ref[...], window, preferred_element_type=F32)
        total = None
        for cell in range(8):
            value = pre[C1 * cell : C1 * cell + C1].astype(BF16)
            bent = jnp.tanh(value)
            gate = bent + 0.65 / 0.35
            act = value * gate
            slope_ref[row * 8 + cell, :, lanes] = gate + value * (1.0 - bent * bent)
            total = act if total is None else total + act
        pooled_ref[row * C1 : row * C1 + C1, lanes] = (
            total.astype(F32) * (0.125 * 0.35)
        ).astype(BF16)

    for tile in range(CELLS // TILE):
        lanes = slice(tile * TILE, tile * TILE + TILE)
        wide_ref[:, lanes] = jnp.dot(forward_ref[...], pooled_ref[:, lanes], preferred_element_type=F32)
    depth = depth_of((16, CELLS))
    for block in range(4):
        def term(dy, dz):
            at = 64 * (3 * dy + dz) + 16 * block
            return wide_ref[at : at + 16, :]

        def column(dz):
            return term(1, dz) + move(term(0, dz), HZ) + move(term(2, dz), -HZ)

        pre = column(1) + from_below(column(0), depth) + from_above(column(2), depth)
        rows = slice(16 * block, 16 * block + 16)
        bent = jnp.tanh(pre)
        gate = 0.65 + 0.35 * bent
        feature_ref[rows, :] = (pre * gate).astype(BF16)
        slope = gate + 0.35 * pre * (1.0 - bent * bent)
        grads = (cot_ref[rows, :].astype(F32) * slope).astype(BF16).astype(F32)
        for dy in range(3):
            here = grads if dy == 1 else move(grads, HZ * (dy - 1))
            for dz in range(3):
                there = here if dz == 1 else (from_above if dz == 0 else from_below)(here, depth)
                at = 64 * (3 * dy + dz) + 16 * block
                moved_ref[at : at + 16, :] = there.astype(BF16)
    for tile in range(CELLS // TILE):
        lanes = slice(tile * TILE, tile * TILE + TILE)
        back_ref[:, lanes] = jnp.dot(
            backward_ref[...], moved_ref[:, lanes], preferred_element_type=F32
        ).astype(BF16)
    grad = lax.dot_general(
        moved_ref[...], pooled_ref[...], (((1,), (1,)), ((), ())), preferred_element_type=F32
    )
    for tap in range(9):
        both = grad[64 * tap : 64 * tap + 32, :192] + grad[64 * tap + 32 : 64 * tap + 64, 64:]
        keep = jnp.where(side == 0, both[:16], both[16:])
        send = jnp.where(side == 0, both[16:], both[:16])
        for dx in range(3):
            at = dx * 576 + tap * 64
            keep_ref[:, at : at + 64] = keep[:, 64 * dx : 64 * dx + 64]
            send_ref[:, at : at + 64] = send[:, 64 * dx : 64 * dx + 64]
    sum_ref[...] = jnp.zeros_like(sum_ref)

    def back_step(row, _):
        window = windows_ref[pl.ds(pl.multiple_of(row * 128, 128), 256), :]
        back = back_ref[pl.ds(pl.multiple_of(row * C1, C1), C1), :]
        grads = jnp.concatenate([slope_ref[row * 8 + cell] * back for cell in range(8)], axis=0)
        sum_ref[...] += lax.dot_general(
            grads, window, (((1,), (1,)), ((), ())), preferred_element_type=F32
        )
        return 0

    lax.fori_loop(0, ROWS, back_step, 0, unroll=2)
    total = jnp.zeros((C1, 128), F32)
    for cell in range(8):
        whole = sum_ref[C1 * cell : C1 * cell + C1, :]
        high = whole.astype(BF16)
        low = (whole - high.astype(F32)).astype(BF16)
        total += jnp.dot(high, taps_ref[cell], preferred_element_type=F32)
        total += jnp.dot(low, taps_ref[cell], preferred_element_type=F32)
    total = total * (0.125 * 0.35)
    keep_one_ref[...] = jnp.where(side == 0, total[:32], total[32:])
    send_one_ref[...] = jnp.where(side == 0, total[32:], total[:32])


def levels(side, own, other, fine, forward, backward, cot, taps):
    whole = pl.BlockSpec(memory_space=pltpu.VMEM)
    return pl.pallas_call(
        levels_kernel,
        in_specs=[pl.BlockSpec(memory_space=pltpu.SMEM)]
        + [whole] * 7,
        out_specs=[whole] * 5,
        out_shape=[
            jax.ShapeDtypeStruct((64, CELLS), BF16),
            jax.ShapeDtypeStruct((16, 1728), F32),
            jax.ShapeDtypeStruct((16, 1728), F32),
            jax.ShapeDtypeStruct((32, 128), F32),
            jax.ShapeDtypeStruct((32, 128), F32),
        ],
        scratch_shapes=[
            pltpu.VMEM((640, CELLS), BF16),
            pltpu.VMEM((32, C1, CELLS), BF16),
            pltpu.VMEM((ROWS * C1, CELLS), BF16),
            pltpu.VMEM((576, CELLS), F32),
            pltpu.VMEM((576, CELLS), BF16),
            pltpu.VMEM((ROWS * C1, CELLS), BF16),
            pltpu.VMEM((512, 256), F32),
        ],
        compiler_params=pltpu.CompilerParams(vmem_limit_bytes=48 << 20),
        name="levels",
    )(side, own, other, fine, forward, backward, cot, taps)


def swap(values):
    return lax.ppermute(values, "core", [(0, 1), (1, 0)])


def by_core(side, mine, other, dim):
    return jnp.where(
        side == 0, jnp.concatenate([mine, other], dim), jnp.concatenate([other, mine], dim)
    )


def strip_parts(density):
    whole = pl.BlockSpec(memory_space=pltpu.VMEM)
    copies = pl.pallas_call(
        sort_kernel,
        in_specs=[whole],
        out_specs=whole,
        out_shape=jax.ShapeDtypeStruct((8, 128, 256), BF16),
        compiler_params=pltpu.CompilerParams(vmem_limit_bytes=8 << 20),
        name="sort_block",
    )(density)
    column = lax.all_to_all(copies, ("x", "zh"), 0, 0)
    strips = jnp.concatenate(
        [jnp.roll(column[:, 80:], 1, 0), column, jnp.roll(column[:, :48], -1, 0)], axis=1
    )
    return lax.all_to_all(strips, ("zl", "y"), 0, 0)


def coarse_weights(weight_two):
    taps = weight_two.reshape(32, 3, 9, C1)
    both = jnp.stack([jnp.pad(taps, ((0, 0), (r, 1 - r), (0, 0), (0, 0))) for r in range(2)])
    forward = both.transpose(3, 0, 1, 2, 4).reshape(576, 256)
    return forward, forward.T


def ring(count, step):
    return [(i, (i + step) % count) for i in range(count)]


def sum_one(keep, send, features, side):
    mine = (keep + swap(send)).astype(BF16)
    copies = jnp.broadcast_to(mine[None], (64, 32, 128))
    terms = lax.all_to_all(copies, CHIP[:4], 0, 0)
    terms, features = lax.optimization_barrier((terms, features))
    half = terms.astype(F32).sum(0)
    return by_core(side, half, swap(half), 0)[:, :108], features


def sum_two(keep, send, side):
    mine = (keep + swap(send)).astype(BF16)
    mine = (mine.astype(F32) + lax.ppermute(mine, "zl", ring(2, 1)).astype(F32)).astype(BF16)
    terms = [lax.ppermute(mine, "y", ring(4, step)).astype(F32) for step in (2, 1, 3)]
    half = mine.astype(F32) + terms[0] + terms[1] + terms[2]
    return by_core(side, half, swap(half), 0)


def body(density, weight_one, weight_two, feature_cot):
    taps = jnp.asarray(window_taps(), BF16)
    side = lax.axis_index("core")
    with jax.named_scope("strip"):
        own = strip_parts(density)
    with jax.named_scope("weights"):
        fine_weight = jnp.einsum(
            "ok,srk->sor", jnp.pad(weight_one, ((0, 0), (0, 20))), taps, preferred_element_type=F32
        ).astype(BF16).reshape(512, 256)
        forward, backward = coarse_weights(weight_two)
        cot = feature_cot.transpose(1, 0, 2).reshape(64, CELLS)
    own, fine_weight, forward, backward, cot = lax.optimization_barrier(
        (own, fine_weight, forward, backward, cot)
    )
    features, keep, send, keep_one, send_one = levels(
        side.astype(jnp.int32).reshape(1), own, swap(own), fine_weight, forward, backward, cot, taps
    )
    features = features.reshape(2, 32, CELLS).transpose(1, 0, 2)
    with jax.named_scope("sums"):
        grad_one, features = sum_one(keep_one, send_one, features, side)
        grad_two = sum_two(keep, send, side)
    return features, grad_one, grad_two


def solution(mesh):
    fine_mesh = Mesh(mesh.devices.reshape(4, 2, 2, 4, 2), CHIP)
    gx, gy = ("x", "zh"), ("zl", "y", "core")
    return jax.shard_map(
        body,
        mesh=fine_mesh,
        in_specs=(P(None, gx, gy), P(), P(gx, None), P(gx, gy, None)),
        out_specs=(P(gx, gy, None), P(), P(gx, None)),
        check_vma=False,
    )
```
